128 devices in a mesh: seq: 16 (over y_lo, x, core), aud: 8 (over y_hi, z).
Axes of the slice: x: 4, y: 4 (y_hi: 2, y_lo: 2; y = y_hi * 2 + y_lo), z: 4, core: 2. Of those that a mesh axis runs over, the one named last changes fastest.
Arguments:
- video_q: bfloat16 [8192, 3072], P('seq', 'aud'), may hold values from -18 to 18
- video_k: bfloat16 [8192, 3072], P('seq', 'aud'), may hold values from -4.5 to 4.5
- video_v: bfloat16 [8192, 3072], P('seq', 'aud'), may hold values from -6 to 6
- audio_k: bfloat16 [512, 3072], P('aud'), may hold values from -4.5 to 4.5
- audio_v: bfloat16 [512, 3072], P('aud'), may hold values from -6 to 6
- text_k: bfloat16 [512, 3072], P('seq', 'aud'), may hold values from -4.5 to 4.5
- text_v: bfloat16 [512, 3072], P('seq', 'aud'), may hold values from -6 to 6
- block_start: int32 [64], P('seq'), may hold values from 0 to 510, as said below
- block_len: int32 [64], P('seq'), may hold values from 2 to 128, as said below
- prompt_len: int32 [1], replicated, may hold values from 128 to 512
- w_out: bfloat16 [3072, 3072], P('aud'), may hold values from -0.109375 to 0.109375
Outputs:
- video_out: bfloat16 [8192, 3072], P(('seq', 'aud'))
The draws below stay inside these ranges and needn't reach their ends.
Inputs may be any that keep to these rules, and one draw needn't show every extreme that they name: block_start[b] + block_len[b] <= 512 for every block b; with c = b * 8 + 512 // 128, block b's window lies within audio tokens c - 128 to c + 128: block_start[b] >= c - 128 and block_start[b] + block_len[b] <= c + 128. `block_len`: some block's window holds exactly 128 audio tokens.
All inputs are finite; a program needn't handle non-finite values.
Results may differ from the reference program's by a relative error of at most 0.017.
Values may be sent and summed in bfloat16 or wider, within the bound.
No kernel may reach another device: no remote copies, remote signals or barrier semaphores. Data moves between devices by JAX's collectives and lax.ppermute only.
A program may use at most 128 MiB of HBM per device.

```python
import jax
import jax.numpy as jnp
from jax import lax

D = 3072
HEADS = 24
HD = 128
TXT = 512
VBLK = 128
WIN = 128
VTOK = 8192
ATOK = 512
NB = 64


def intersection_lists(key):
    key = jax.random.fold_in(key, 101)
    key_one, key_two, key_three = jax.random.split(key, 3)
    widths = jax.random.randint(key_one, (NB,), 2, WIN + 1)
    longest = jax.random.randint(key_two, (), 0, NB - 1)
    blocks = jnp.arange(NB, dtype=jnp.int32)
    widths = jnp.where(blocks == longest, WIN, widths)
    widths = jnp.where(blocks == NB - 1, 2, widths)
    centre = blocks * ATOK // NB + ATOK // (2 * NB)
    jitter = jax.random.randint(key_three, (NB,), -(WIN // 4), WIN // 4 + 1)
    starts = jnp.clip(centre - widths // 2 + jitter, 0, ATOK - widths)
    starts = jnp.where(blocks == NB - 1, ATOK - 2, starts)
    return (starts.astype(jnp.int32), widths.astype(jnp.int32))


def query_rows():
    return [number * (VTOK // 4) + 5 for number in range(4)]


def base_rows(key, constant, row_count):
    key = jax.random.fold_in(key, constant)
    key_one = jax.random.fold_in(key, 0)
    normal = jax.random.normal(key_one, (row_count, D), jnp.float32)
    return jnp.clip(normal, -4.0, 4.0)


def lift_pairs(entries, positions, raising):
    for position in positions:
        strong = entries[position]
        entries = entries.at[position].set(strong)
        entries = entries.at[position + 1].set(jnp.where(raising > 1.0, 0.99 * strong, entries[position + 1]))
    return entries


def video_key_table(key, raising):
    positions = [(number + VTOK // 2) % VTOK for number in query_rows()]
    return lift_pairs(base_rows(key, 211, VTOK), positions, raising)


def text_key_table(key, raising):
    positions = [2 * number for number in range(4)]
    return lift_pairs(base_rows(key, 223, TXT), positions, raising)


def audio_key_table(key, raising):
    starts, widths = intersection_lists(key)
    positions = [starts[(number + 2) // VBLK] for number in query_rows()]
    return lift_pairs(base_rows(key, 227, ATOK), positions, raising)


def draw_block_start(key, part):
    starts, widths = intersection_lists(key)
    return starts


def draw_block_len(key, part):
    starts, widths = intersection_lists(key)
    return widths


def draw_video_k(key, part):
    raising = 1.0
    return video_key_table(key, raising).astype(jnp.bfloat16)


def draw_text_k(key, part):
    raising = 1.0
    return text_key_table(key, raising).astype(jnp.bfloat16)


def draw_audio_k(key, part):
    raising = 1.0
    return audio_key_table(key, raising).astype(jnp.bfloat16)


def draw_video_q(key, part):
    raising = 1.0
    video_keys = video_key_table(key, raising)
    text_keys = text_key_table(key, raising)
    audio_keys = audio_key_table(key, raising)
    starts, widths = intersection_lists(key)
    key = jax.random.fold_in(key, 7)
    entries = 2.5 * base_rows(key, 229, VTOK)
    strengths = (1.6, 2.4, 3.2, 4.0)
    for number, target in enumerate(query_rows()):
        entries = entries.at[target].set(strengths[number] * video_keys[(target + VTOK // 2) % VTOK])
        entries = entries.at[target + 1].set(strengths[number] * text_keys[2 * number])
        entries = entries.at[target + 2].set(strengths[number] * audio_keys[starts[(target + 2) // VBLK]])
    return entries.astype(jnp.bfloat16)


def levels(own_key, extent, cuts, smallest, largest):
    gain, own = 1.0, jax.random.fold_in(own_key, 6)
    for dim, shards_of in cuts:
        heights = jnp.exp(jax.random.uniform(jax.random.fold_in(own, dim), (shards_of,), jnp.float32, smallest / len(cuts), largest / len(cuts)))
        gain = gain * jnp.repeat(heights, extent[dim] // shards_of).reshape([-1 if axis == dim else 1 for axis in range(len(extent))])
    return gain


def scatter_about(stream_key, dims, scale, most, cuts=(), held_as=jnp.bfloat16):
    drawn = jax.random.normal(stream_key, dims, jnp.float32) * scale
    if len(cuts) > 0:
        drawn = levels(stream_key, dims, cuts, -0.22, 0.18) * drawn
    return jnp.clip(drawn, min=-most, max=most).astype(held_as)


def setup_inputs(seed: int = 0) -> dict:
    arg_keys = jax.random.split(jax.random.key(seed), 12)
    return {
        "video_q": draw_video_q(jax.random.fold_in(arg_keys[11], 71), 0),
        "video_k": draw_video_k(jax.random.fold_in(arg_keys[11], 71), 0),
        "video_v": scatter_about(arg_keys[2], (VTOK, D), 1.0, 6.0, ((0, 16), (1, 8))),
        "audio_k": draw_audio_k(jax.random.fold_in(arg_keys[11], 71), 0),
        "audio_v": scatter_about(arg_keys[4], (ATOK, D), 1.0, 6.0, ((0, 8),)),
        "text_k": draw_text_k(jax.random.fold_in(arg_keys[11], 71), 0),
        "text_v": scatter_about(arg_keys[6], (TXT, D), 1.0, 6.0, ((0, 16), (1, 8))),
        "block_start": draw_block_start(jax.random.fold_in(arg_keys[11], 71), 0),
        "block_len": draw_block_len(jax.random.fold_in(arg_keys[11], 71), 0),
        "prompt_len": jax.random.randint(arg_keys[9], (1,), TXT // 4, TXT + 1).astype(jnp.int32),
        "w_out": scatter_about(arg_keys[10], (D, D), D ** -0.5, 0.109375, ((0, 8),)),
    }


def heads_of(matrix):
    return matrix.reshape(matrix.shape[0], HEADS, HD)


def attend(queries, key_rows, value_rows, allowed):
    scores = jnp.einsum('qhd,khd->hqk', queries.astype(jnp.float32), key_rows.astype(jnp.float32)) * (HD ** -0.5)
    if allowed is not None:
        scores = jnp.where(allowed[None, None, :], scores, -1e30)
    peak_score = jnp.max(scores, axis=-1, keepdims=True)
    weights = jnp.exp(scores - peak_score)
    weight_sum = jnp.sum(weights, axis=-1)
    rounded = weights.astype(jnp.bfloat16)
    mixture = jnp.einsum('hqk,khd->hqd', rounded.astype(jnp.float32), value_rows.astype(jnp.float32))
    mixture = mixture / weight_sum[..., None]
    return jnp.transpose(mixture, (1, 0, 2)).reshape(queries.shape[0], -1)


def reference(video_q, video_k, video_v, audio_k, audio_v, text_k, text_v, block_start, block_len, prompt_len, w_out):
    queries = heads_of(video_q).reshape(NB, VBLK, HEADS, HD)
    video_keys = heads_of(video_k)
    video_vals = heads_of(video_v)
    audio_keys = heads_of(audio_k)
    audio_vals = heads_of(audio_v)
    text_keys = heads_of(text_k)
    text_vals = heads_of(text_v)
    spoken = jnp.arange(TXT, dtype=jnp.int32) < prompt_len[0]

    def one_block(blocked):
        block_q, window_start, window_len = blocked
        offset = jnp.minimum(window_start, ATOK - WIN).astype(jnp.int32)
        near_keys = lax.dynamic_slice_in_dim(audio_keys, offset, WIN, 0)
        near_vals = lax.dynamic_slice_in_dim(audio_vals, offset, WIN, 0)
        key_index = offset + jnp.arange(WIN, dtype=jnp.int32)
        inside = (key_index >= window_start) & (key_index < window_start + window_len)
        self_part = attend(block_q, video_keys, video_vals, None)
        audio_part = attend(block_q, near_keys, near_vals, inside)
        text_part = attend(block_q, text_keys, text_vals, spoken)
        return (self_part + audio_part + text_part).astype(jnp.bfloat16)

    joined_heads = lax.map(one_block, (queries, block_start, block_len)).reshape(VTOK, D)
    return jnp.dot(joined_heads, w_out, preferred_element_type=jnp.float32).astype(jnp.bfloat16)
```

```python
import functools
import itertools

import jax
import jax.numpy as jnp
from jax import lax
from jax.experimental import pallas as pl
from jax.experimental.pallas import tpu as pltpu
from jax.sharding import PartitionSpec as P

HD = 128
HEADS = 3
GROUP = HEADS * HD
SUB = 256
SCALE = HD ** (-0.5) * 1.4426950408889634
DEAD = -1e30
AXES = ("seq", "aud")
NT = (((1,), (1,)), ((), ()))
NN = (((1,), (0,)), ((), ()))
F32 = jnp.float32
BF16 = jnp.bfloat16
PARAMS = pltpu.CompilerParams(vmem_limit_bytes=32 * 2**20)


def pairs(move):
    index = lambda yl, x, c, yh, z: ((yl * 4 + x) * 2 + c) * 8 + yh * 4 + z
    places = itertools.product(range(2), range(4), range(2), range(2), range(4))
    return [(index(*place), index(*move(*place))) for place in places]


X_UP = pairs(lambda yl, x, c, yh, z: (yl, (x + 1) % 4, c, yh, z))
X_DOWN = pairs(lambda yl, x, c, yh, z: (yl, (x - 1) % 4, c, yh, z))
Y_LO = pairs(lambda yl, x, c, yh, z: (1 - yl, x, c, yh, z))
Y_HI = pairs(lambda yl, x, c, yh, z: (yl, x, c, 1 - yh, z))
CORE = pairs(lambda yl, x, c, yh, z: (yl, x, 1 - c, yh, z))
Z_RINGS = [[0, 1, 2, 3], [4, 5, 6, 7]]


def send(array, route):
    return lax.ppermute(array, AXES, route)


def with_ones(values):
    return jnp.concatenate([values, jnp.ones((values.shape[0], HD), BF16)], axis=1)


def flash_body(pieces, first, last, n_arrays, n_sets, *refs):
    arrays = refs[:n_arrays]
    refs = refs[n_arrays:]
    queries = refs[:n_sets]
    refs = refs[n_sets:]
    states = None
    if not first:
        states = refs[: 2 * n_sets]
        refs = refs[2 * n_sets :]
    outs = refs
    for number in range(n_sets):
        q_ref = queries[number]
        for start in range(0, q_ref.shape[0], SUB):
            rows = pl.ds(start, SUB)
            stats = []
            for head in range(HEADS):
                cols = pl.ds(head * HD, HD)
                vcols = pl.ds(GROUP + head * HD, HD)
                q = q_ref[rows, cols]
                scores = []
                peak = None
                if not first:
                    acc_ref, stat_ref = states[2 * number], states[2 * number + 1]
                    old_peak = stat_ref[rows, 2 * head : 2 * head + 1]
                    old_sum = stat_ref[rows, 2 * head + 1 : 2 * head + 2]
                    peak = old_peak
                for which, offset, count in pieces:
                    k = arrays[which][pl.ds(offset, count), cols]
                    s = lax.dot_general(q, k, NT, preferred_element_type=F32) * SCALE
                    scores.append(s)
                    top = jnp.max(s, axis=1, keepdims=True)
                    peak = top if peak is None else jnp.maximum(peak, top)
                total = None
                for s, (which, offset, count) in zip(scores, pieces):
                    p = jnp.exp2(s - peak).astype(BF16)
                    v = with_ones(arrays[which][pl.ds(offset, count), vcols])
                    part = lax.dot_general(p, v, NN, preferred_element_type=F32)
                    total = part if total is None else total + part
                acc = total[:, :HD]
                weight = total[:, HD : HD + 1]
                if not first:
                    shrink = jnp.exp2(old_peak - peak)
                    acc = acc + acc_ref[rows, cols] * shrink
                    weight = weight + old_sum * shrink
                if last:
                    outs[2 * number][rows, cols] = (acc / weight).astype(outs[2 * number].dtype)
                    stats += [peak + jnp.log2(weight)]
                else:
                    outs[2 * number][rows, cols] = acc
                    stats += [peak, weight]
            lane = lax.broadcasted_iota(jnp.int32, (SUB, HD), 1)
            packed = jnp.zeros((SUB, HD), F32)
            for place, column in enumerate(stats):
                packed = jnp.where(lane == place, column, packed)
            outs[2 * number + 1][rows, :] = packed


def flash(name, arrays, pieces, queries, states, last):
    first = states is None
    rows = queries[0].shape[0]
    n_sets = len(queries)
    keys = sum(count for _, _, count in pieces)
    shapes = []
    for _ in range(n_sets):
        shapes += [
            jax.ShapeDtypeStruct((rows, GROUP), BF16 if last else F32),
            jax.ShapeDtypeStruct((rows, HD), F32),
        ]
    flat = [] if first else [part for state in states for part in state]
    outs = pl.pallas_call(
        functools.partial(flash_body, pieces, first, last, len(arrays), n_sets),
        out_shape=shapes,
        compiler_params=PARAMS,
        cost_estimate=pl.CostEstimate(
            flops=8 * n_sets * rows * keys * GROUP,
            bytes_accessed=sum(a.size * 2 for a in arrays) + 4 * n_sets * rows * GROUP,
            transcendentals=n_sets * rows * keys * HEADS,
        ),
        name=name,
    )(*arrays, *queries, *flat)
    return [(outs[2 * i], outs[2 * i + 1]) for i in range(n_sets)]


def side_body(start_ref, length_ref, q_ref, text_a, text_b, live_ref, audio_ref, out_ref):
    audio_rows = audio_ref.shape[0] // 16
    for head in range(HEADS):
        cols = pl.ds(head * HD, HD)
        vcols = pl.ds(GROUP + head * HD, HD)
        text_k = jnp.concatenate([text_a[:, cols], text_b[:, cols]], axis=0)
        text_v = with_ones(jnp.concatenate([text_a[:, vcols], text_b[:, vcols]], axis=0))
        parts_k = [audio_ref[pl.ds(2 * i * audio_rows, audio_rows), cols] for i in range(8)]
        parts_v = [audio_ref[pl.ds((2 * i + 1) * audio_rows, audio_rows), cols] for i in range(8)]
        audio_k = jnp.concatenate(parts_k, axis=0)
        audio_v = with_ones(jnp.concatenate(parts_v, axis=0))
        for block in range(q_ref.shape[0] // HD):
            rows = pl.ds(block * HD, HD)
            q = q_ref[rows, cols]
            s = lax.dot_general(q, text_k, NT, preferred_element_type=F32) * SCALE
            s = jnp.where(live_ref[...] > 0, s, DEAD)
            p = jnp.exp2(s - jnp.max(s, axis=1, keepdims=True)).astype(BF16)
            mix = lax.dot_general(p, text_v, NN, preferred_element_type=F32)
            s = lax.dot_general(q, audio_k, NT, preferred_element_type=F32) * SCALE
            place = lax.broadcasted_iota(jnp.int32, s.shape, 1)
            begin = start_ref[block]
            inside = (place >= begin) & (place < begin + length_ref[block])
            s = jnp.where(inside, s, DEAD)
            p = jnp.exp2(s - jnp.max(s, axis=1, keepdims=True)).astype(BF16)
            heard = lax.dot_general(p, audio_v, NN, preferred_element_type=F32)
            out_ref[rows, cols] = heard[:, :HD] / heard[:, HD:] + mix[:, :HD] / mix[:, HD:]


def side(block_start, block_len, q, text_a, text_b, live, audio):
    smem = pl.BlockSpec(memory_space=pltpu.SMEM)
    vmem = pl.BlockSpec(memory_space=pltpu.VMEM)
    return pl.pallas_call(
        side_body,
        out_shape=jax.ShapeDtypeStruct(q.shape, F32),
        in_specs=[smem, smem] + [vmem] * 5,
        out_specs=vmem,
        compiler_params=PARAMS,
        cost_estimate=pl.CostEstimate(
            flops=8 * q.shape[0] * 1024 * GROUP, bytes_accessed=4 * 2**20, transcendentals=0
        ),
        name="side",
    )(block_start, block_len, q, text_a, text_b, live, audio)


def split_three(column):
    high = column.astype(BF16)
    rest = column - high.astype(F32)
    mid = rest.astype(BF16)
    low = (rest - mid.astype(F32)).astype(BF16)
    return high, mid, low


def pack_body(out_ref, lse_ref, packed_ref):
    packed_ref[:, :GROUP] = out_ref[...]
    lse = lse_ref[...]
    high, mid, low = split_three(lse)
    lane = lax.broadcasted_iota(jnp.int32, lse.shape, 1)
    table = jnp.zeros(lse.shape, F32)
    for number, piece in enumerate((high, mid, low)):
        for head in range(HEADS):
            column = piece[:, head : head + 1].astype(F32)
            table = jnp.where(lane == number * HEADS + head, column, table)
    packed_ref[:, GROUP:] = table.astype(BF16)


def pack(out, lse):
    return pl.pallas_call(
        pack_body,
        out_shape=jax.ShapeDtypeStruct((out.shape[0], GROUP + HD), BF16),
        compiler_params=PARAMS,
        name="pack",
    )(out, lse)


def merge_body(mine_ref, lse_ref, packed_ref, side_ref, joined_ref):
    lse = lse_ref[...]
    table = packed_ref[:, GROUP:].astype(F32)
    for head in range(HEADS):
        cols = pl.ds(head * HD, HD)
        own = lse[:, head : head + 1]
        other = table[:, head : head + 1]
        for number in (1, 2):
            place = number * HEADS + head
            other = other + table[:, place : place + 1]
        peak = jnp.maximum(own, other)
        w_own = jnp.exp2(own - peak)
        w_other = jnp.exp2(other - peak)
        mixed = mine_ref[:, cols].astype(F32) * w_own + packed_ref[:, cols].astype(F32) * w_other
        joined_ref[:, cols] = (mixed / (w_own + w_other) + side_ref[:, cols]).astype(BF16)


def merge(mine, lse, packed, side_part):
    return pl.pallas_call(
        merge_body,
        out_shape=jax.ShapeDtypeStruct(mine.shape, BF16),
        compiler_params=PARAMS,
        name="merge",
    )(mine, lse, packed, side_part)


def on_device(
    video_q,
    video_k,
    video_v,
    audio_k,
    audio_v,
    text_k,
    text_v,
    block_start,
    block_len,
    prompt_len,
    w_out,
):
    seq = lax.axis_index("seq")
    core = seq % 2
    half = w_out.shape[1] // 2
    w_half = lax.dynamic_slice_in_dim(w_out, core * half, half, axis=1)
    w_ring = lax.all_gather(w_half, "aud", axis=0, tiled=True, axis_index_groups=Z_RINGS)

    top = jnp.concatenate([video_k[:256], text_k, video_k[256:]], axis=0)
    own = jnp.concatenate(
        [top, jnp.concatenate([video_v[:256], text_v, video_v[256:]], axis=0)], axis=1
    )
    up1 = send(own, X_UP)
    down1 = send(own, X_DOWN)
    other_q = send(video_q, Y_LO)
    own_c = send(own, CORE)
    up2 = send(up1[:272], X_UP)
    down2 = send(down1[272:], X_DOWN)
    audio = lax.all_to_all(
        jnp.concatenate([audio_k, audio_v], axis=0), "aud", split_axis=1, concat_axis=0, tiled=True
    )
    up1_c = send(up1, CORE)
    down1_c = send(down1, CORE)
    up2_c = send(up2, CORE)
    down2_c = send(down2, CORE)

    whole = lambda number: [(number, 0, 256), (number, 288, 256)]
    pieces_near = whole(0) + whole(1)
    (state_other,) = flash("near_other", [own, own_c], pieces_near, [other_q], None, False)
    (state_mine,) = flash("near_mine", [own, own_c], pieces_near, [video_q], None, False)
    arrays = [up1, down1, up1_c, down1_c]
    pieces_mid = whole(0) + whole(1) + whole(2) + whole(3)
    state_other, state_mine = flash(
        "mid", arrays, pieces_mid, [other_q, video_q], [state_other, state_mine], False
    )
    arrays = [up2, down2, up2_c, down2_c]
    pieces_far = [(0, 0, 256), (1, 16, 256), (2, 0, 256), (3, 16, 256)]
    ((part_other, lse_other),) = flash("far_other", arrays, pieces_far, [other_q], [state_other], True)
    got = send(pack(part_other, lse_other), Y_LO)
    ((part_mine, lse_mine),) = flash("far_mine", arrays, pieces_far, [video_q], [state_mine], True)

    text_x = jnp.concatenate(
        [own[256:288], up1[256:288], down1[256:288], up2[256:272], down2[:16]], axis=0
    )
    text_y = send(text_x, Y_LO)
    text_here = jnp.concatenate([text_x, text_y], axis=0)
    text_there = send(text_here, CORE)
    y_lo, x = seq // 8, (seq // 2) % 4
    order = []
    for core_there in (core, 1 - core):
        for y_there in (y_lo, 1 - y_lo):
            for shift in (0, 3, 1, 2):
                order.append(y_there * 8 + ((x + shift) % 4) * 2 + core_there)
    rows_text = text_k.shape[0]
    place = jnp.stack(order)[:, None] * rows_text + jnp.arange(rows_text, dtype=jnp.int32)[None, :]
    live = (place.reshape(1, -1) < prompt_len[0]).astype(F32)
    side_part = side(block_start, block_len, video_q, text_here, text_there, live, audio)
    joined = merge(part_mine, lse_mine, got, side_part)

    out_rows = joined.shape[0] // 8
    ready = joined.reshape(2, 4, out_rows, GROUP).transpose(1, 0, 2, 3).reshape(4, -1, GROUP)
    ring = lax.all_to_all(
        ready, "aud", split_axis=0, concat_axis=0, tiled=True, axis_index_groups=Z_RINGS
    )
    ring_c = send(ring, CORE)
    both = jnp.concatenate([ring, ring_c], axis=1)
    both = both.transpose(1, 0, 2).reshape(-1, 4 * GROUP)
    partial = jnp.dot(both, w_ring, preferred_element_type=F32)
    partial = partial.reshape(2, 2, out_rows, half)
    y_hi = lax.axis_index("aud") // 4
    mine = lax.dynamic_index_in_dim(partial, y_hi, axis=1, keepdims=False)
    theirs = lax.dynamic_index_in_dim(partial, 1 - y_hi, axis=1, keepdims=False)
    summed = (mine + send(theirs.astype(BF16), Y_HI).astype(F32)).astype(BF16)
    here = summed[0]
    there = send(summed[1], CORE)
    left = jnp.where(core == 0, here, there)
    right = jnp.where(core == 0, there, here)
    return jnp.concatenate([left, right], axis=1)


def solution(mesh):
    placed = (
        P("seq", "aud"),
        P("seq", "aud"),
        P("seq", "aud"),
        P("aud", None),
        P("aud", None),
        P("seq", "aud"),
        P("seq", "aud"),
        P("seq"),
        P("seq"),
        P(),
        P("aud", None),
    )
    return jax.shard_map(
        on_device, mesh=mesh, in_specs=placed, out_specs=P(("seq", "aud"), None), check_vma=False
    )
```

```python
import functools
import itertools

import jax
import jax.numpy as jnp
from jax import lax
from jax.experimental import pallas as pl
from jax.experimental.pallas import tpu as pltpu
from jax.sharding import PartitionSpec as P

HD = 128
HEADS = 3
GROUP = HEADS * HD
SUB = 256
ROWS = 512
TEXT = 32
SCALE = HD ** (-0.5) * 1.4426950408889634
DEAD = -1e30
AXES = ("seq", "aud")
NT = (((1,), (1,)), ((), ()))
NN = (((1,), (0,)), ((), ()))
F32 = jnp.float32
BF16 = jnp.bfloat16
PARAMS = pltpu.CompilerParams(vmem_limit_bytes=20 * 2**20)
WIDE = pltpu.CompilerParams(vmem_limit_bytes=60 * 2**20)
COST = pl.CostEstimate(flops=1024, bytes_accessed=1024, transcendentals=0)


def lasting(us):
    return pl.CostEstimate(flops=int(us * 1.15e9), bytes_accessed=1024, transcendentals=0)


TIMES = dict(near_mine=2.4, near_other=2.4, mid=8.0, far_other=2.8, far_mine=26.0, side=2.7)
SMEM = pl.BlockSpec(memory_space=pltpu.SMEM)
VMEM = pl.BlockSpec(memory_space=pltpu.VMEM)
HBM = pl.BlockSpec(memory_space=pltpu.HBM)


def pairs(move):
    index = lambda yl, x, c, yh, z: ((yl * 4 + x) * 2 + c) * 8 + yh * 4 + z
    places = itertools.product(range(2), range(4), range(2), range(2), range(4))
    return [(index(*place), index(*move(*place))) for place in places]


X_A = pairs(lambda yl, x, c, yh, z: (yl, (x + 1 - 2 * c) % 4, c, yh, z))
X_B = pairs(lambda yl, x, c, yh, z: (yl, (x - 1 + 2 * c) % 4, c, yh, z))
Z_A = pairs(lambda yl, x, c, yh, z: (yl, x, c, yh, (z + 1 - 2 * c) % 4))
Z_B = pairs(lambda yl, x, c, yh, z: (yl, x, c, yh, (z - 1 + 2 * c) % 4))
Z_2 = pairs(lambda yl, x, c, yh, z: (yl, x, c, yh, (z + 2) % 4))
Y_LO = pairs(lambda yl, x, c, yh, z: (1 - yl, x, c, yh, z))
Y_NEAR = pairs(lambda yl, x, c, yh, z: (1 - yl, x, c, 1 - yh, z))
Y_HI = pairs(lambda yl, x, c, yh, z: (yl, x, c, 1 - yh, z))
CORE = pairs(lambda yl, x, c, yh, z: (yl, x, 1 - c, yh, z))
Y_HI_CORE = pairs(lambda yl, x, c, yh, z: (yl, x, 1 - c, 1 - yh, z))


def send(array, route):
    return lax.ppermute(array, AXES, route)


def after(value, *others):
    return lax.optimization_barrier((value,) + others)[0]


def with_ones(values):
    return jnp.concatenate([values, jnp.ones((values.shape[0], HD), BF16)], axis=1)


def move(sem, *pairs_of_refs):
    copies = [pltpu.make_async_copy(*pair, sem.at[i]) for i, pair in enumerate(pairs_of_refs)]
    for copy in copies:
        copy.start()
    for copy in copies:
        copy.wait()


def stage_body(_, k, v, tk, tv, own, sem):
    left, right = pl.ds(0, GROUP), pl.ds(GROUP, GROUP)
    above, below = pl.ds(0, ROWS), pl.ds(ROWS, TEXT)
    move(
        sem,
        (k, own.at[above, left]),
        (v, own.at[above, right]),
        (tk, own.at[below, left]),
        (tv, own.at[below, right]),
    )


def stage(*parts):
    return pl.pallas_call(
        stage_body,
        out_shape=jax.ShapeDtypeStruct((ROWS + TEXT, 2 * GROUP), BF16),
        in_specs=[SMEM] + [HBM] * 4,
        out_specs=VMEM,
        scratch_shapes=[pltpu.SemaphoreType.DMA((4,))],
        compiler_params=WIDE,
        cost_estimate=COST,
        name="stage",
    )(*parts)


def split_body(here, w, came, own, keep, give):
    width = own.shape[1]
    half = pl.ds(pl.multiple_of(here[0] * width, width), width)
    rest = pl.ds(pl.multiple_of((1 - here[0]) * width, width), width)
    own[...] = w[:, half]
    keep[...] = came[:, half]
    give[...] = came[:, rest]


def split(here, w, came):
    half = jax.ShapeDtypeStruct((w.shape[0], w.shape[1] // 2), BF16)
    return pl.pallas_call(
        split_body,
        out_shape=[half] * 3,
        in_specs=[SMEM, VMEM, VMEM],
        out_specs=[VMEM] * 3,
        compiler_params=PARAMS,
        cost_estimate=COST,
        name="split",
    )(here, w, came)


def lend_body(here, ak, av, out, sem):
    width = out.shape[1]
    rows = ak.shape[0]
    cols = pl.ds(pl.multiple_of((1 - here[3]) * width, width), width)
    move(sem, (ak.at[:, cols], out.at[pl.ds(0, rows)]), (av.at[:, cols], out.at[pl.ds(rows, rows)]))


def lend(here, ak, av):
    return pl.pallas_call(
        lend_body,
        out_shape=jax.ShapeDtypeStruct((2 * ak.shape[0], ak.shape[1] // 2), BF16),
        in_specs=[SMEM, HBM, HBM],
        out_specs=VMEM,
        scratch_shapes=[pltpu.SemaphoreType.DMA((2,))],
        compiler_params=PARAMS,
        cost_estimate=COST,
        name="lend",
    )(here, ak, av)


def prompt_body(*refs):
    for number, ref in enumerate(refs[:-1]):
        refs[-1][pl.ds(number * TEXT, TEXT), :] = ref[...]


BELOW = pl.BlockSpec((TEXT, 2 * GROUP), lambda i: (ROWS // TEXT, 0))


def prompt(*arrays):
    return pl.pallas_call(
        prompt_body,
        out_shape=jax.ShapeDtypeStruct((len(arrays) * TEXT, 2 * GROUP), BF16),
        grid=(1,),
        in_specs=[BELOW] * len(arrays),
        out_specs=VMEM,
        compiler_params=PARAMS,
        cost_estimate=COST,
        name="prompt",
    )(*arrays)


def deal_body(here, ak, av, lent, *outs):
    core, y_hi, z = here[0], here[3], here[4]
    rows = ak.shape[0]
    step = 1 - 2 * core
    for out, shift in zip(outs, (0, step, -step, 2)):
        target = lax.rem(z + shift + 4, 4)
        cols = pl.ds(pl.multiple_of((y_hi * 4 + target) * GROUP, GROUP), GROUP)
        out[:rows, :] = ak[:, cols]
        out[rows : 2 * rows, :] = av[:, cols]
        out[2 * rows :, :] = lent[:, pl.ds(pl.multiple_of(target * GROUP, GROUP), GROUP)]


def deal(here, ak, av, lent):
    return pl.pallas_call(
        deal_body,
        out_shape=[jax.ShapeDtypeStruct((4 * ak.shape[0], GROUP), BF16)] * 4,
        in_specs=[SMEM, VMEM, VMEM, VMEM],
        out_specs=[VMEM] * 4,
        compiler_params=PARAMS,
        cost_estimate=COST,
        name="deal",
    )(here, ak, av, lent)


def digits(column, count):
    out = []
    for _ in range(count):
        digit = column.astype(BF16).astype(F32)
        column = column - digit
        out.append(digit)
    return out


def undigit(table, head, first, count):
    row = lax.broadcasted_iota(jnp.int32, (HD, HD), 0)
    picked = (row % HEADS == head) & (row >= first * HEADS) & (row < (first + count) * HEADS)
    return lax.dot_general(table, picked.astype(F32).astype(BF16), NN, preferred_element_type=F32)


def blend(parts):
    peak = functools.reduce(jnp.maximum, [part[1] for part in parts])
    scales = [jnp.exp2(part[1] - peak) for part in parts]
    mixed = functools.reduce(lambda a, b: a + b, [p[0] * w for p, w in zip(parts, scales)])
    weight = functools.reduce(lambda a, b: a + b, [p[2] * w for p, w in zip(parts, scales)])
    return mixed, peak, weight


def flash_body(n_arrays, n_sets, n_priors, packed, *refs):
    arrays = refs[:n_arrays]
    queries = refs[n_arrays : n_arrays + n_sets]
    refs = refs[n_arrays + n_sets :]
    priors = refs[: 3 * n_sets * n_priors]
    outs = refs[3 * n_sets * n_priors :]
    lane = lax.broadcasted_iota(jnp.int32, (SUB, HD), 1)
    for number in range(n_sets):
        for start in range(0, ROWS, SUB):
            rows = pl.ds(start, SUB)
            table = jnp.zeros((SUB, HD), F32)
            for head in range(HEADS):
                cols = pl.ds(head * HD, HD)
                vcols = pl.ds(GROUP + head * HD, HD)
                q = queries[number][rows, cols]
                scores = []
                peak = None
                for array in arrays:
                    s = lax.dot_general(q, array[:ROWS, cols], NT, preferred_element_type=F32) * SCALE
                    scores.append(s)
                    top = jnp.max(s, axis=1, keepdims=True)
                    peak = top if peak is None else jnp.maximum(peak, top)
                total = None
                for s, array in zip(scores, arrays):
                    p = jnp.exp2(s - peak).astype(BF16)
                    v = with_ones(array[:ROWS, vcols])
                    part = lax.dot_general(p, v, NN, preferred_element_type=F32)
                    total = part if total is None else total + part
                result = (total[:, :HD], jnp.broadcast_to(peak, (SUB, HD)), total[:, HD:])
                if n_priors:
                    parts = [result]
                    for i in range(n_priors):
                        at = 3 * (number * n_priors + i)
                        parts.append(tuple(priors[at + j][rows, cols] for j in range(3)))
                    result = blend(parts)
                if packed:
                    outs[number][rows, cols] = result[0].astype(BF16)
                    for piece, digit in enumerate(digits(result[1], 3) + digits(result[2], 2)):
                        table = jnp.where(lane == piece * HEADS + head, digit, table)
                else:
                    for j in range(3):
                        outs[3 * number + j][rows, cols] = result[j]
            if packed:
                outs[number][rows, GROUP:] = table.astype(BF16)


def flash(name, arrays, queries, priors=None, packed=False):
    n_sets, n_arrays = len(queries), len(arrays)
    priors = priors or [[] for _ in queries]
    n_priors = len(priors[0])
    flat = [ref for parts in priors for part in parts for ref in part]
    if packed:
        shapes = [jax.ShapeDtypeStruct((ROWS, GROUP + HD), BF16)] * n_sets
    else:
        shapes = [jax.ShapeDtypeStruct((ROWS, GROUP), F32)] * (3 * n_sets)
    outs = pl.pallas_call(
        functools.partial(flash_body, n_arrays, n_sets, n_priors, packed),
        out_shape=shapes,
        compiler_params=PARAMS,
        cost_estimate=lasting(TIMES[name]),
        name=name,
    )(*arrays, *queries, *flat)
    return outs if packed else [tuple(outs[3 * i : 3 * i + 3]) for i in range(n_sets)]


def side_body(here, start_ref, length_ref, prompt_ref, q_ref, *refs):
    audios, texts, out_ref = refs[:4], refs[4:14], refs[14]
    core, x, y_lo, y_hi, z = [here[i] for i in range(5)]
    lane = lax.broadcasted_iota(jnp.int32, (1, 16 * TEXT), 1)
    place = jnp.zeros((1, 16 * TEXT), jnp.int32)
    for number in range(16):
        y = y_lo if number < 8 else 1 - y_lo
        c = core if number % 8 < 4 else 1 - core
        step = 2 * c - 1
        shift = (0, step, -step, 2)[number % 4]
        block = y * 8 + lax.rem(x + shift + 4, 4) * 2 + c
        place = jnp.where(lane // TEXT == number, block * TEXT + lane % TEXT, place)
    live = place < prompt_ref[0]
    shard = audios[0].shape[0] // 4
    heard_at = jnp.zeros((1, 8 * shard), jnp.int32)
    lane = lax.broadcasted_iota(jnp.int32, (1, 8 * shard), 1)
    step = 1 - 2 * core
    for number in range(8):
        source = lax.rem(z + (0, -step, step, 2)[number // 2] + 4, 4)
        y = y_hi if number % 2 == 0 else 1 - y_hi
        block = y * 4 + source
        heard_at = jnp.where(lane // shard == number, block * shard + lane % shard, heard_at)
    for head in range(HEADS):
        cols = pl.ds(head * HD, HD)
        vcols = pl.ds(GROUP + head * HD, HD)
        text_k = jnp.concatenate([ref[:, cols] for ref in texts], axis=0)
        text_v = with_ones(jnp.concatenate([ref[:, vcols] for ref in texts], axis=0))
        parts = [(ref, half) for ref in audios for half in (0, 2 * shard)]
        audio_k = jnp.concatenate([ref[pl.ds(half, shard), cols] for ref, half in parts], axis=0)
        audio_v = [ref[pl.ds(half + shard, shard), cols] for ref, half in parts]
        audio_v = with_ones(jnp.concatenate(audio_v, axis=0))
        for block in range(ROWS // HD):
            rows = pl.ds(block * HD, HD)
            q = q_ref[rows, cols]
            s = lax.dot_general(q, text_k, NT, preferred_element_type=F32) * SCALE
            s = jnp.where(live, s, DEAD)
            p = jnp.exp2(s - jnp.max(s, axis=1, keepdims=True)).astype(BF16)
            mix = lax.dot_general(p, text_v, NN, preferred_element_type=F32)
            s = lax.dot_general(q, audio_k, NT, preferred_element_type=F32) * SCALE
            begin = start_ref[block]
            inside = (heard_at >= begin) & (heard_at < begin + length_ref[block])
            s = jnp.where(inside, s, DEAD)
            p = jnp.exp2(s - jnp.max(s, axis=1, keepdims=True)).astype(BF16)
            heard = lax.dot_general(p, audio_v, NN, preferred_element_type=F32)
            out_ref[rows, cols] = heard[:, :HD] / heard[:, HD:] + mix[:, :HD] / mix[:, HD:]


def side(here, block_start, block_len, prompt_len, q, audios, texts, pair_texts):
    return pl.pallas_call(
        side_body,
        out_shape=jax.ShapeDtypeStruct(q.shape, F32),
        grid=(1,),
        in_specs=[SMEM] * 4 + [VMEM] * 5 + [BELOW] * 8 + [VMEM] * 2,
        out_specs=VMEM,
        compiler_params=PARAMS,
        cost_estimate=lasting(TIMES["side"]),
        name="side",
    )(here, block_start, block_len, prompt_len, q, *audios, *texts, *pair_texts)


def join_body(here, *refs):
    mine, packed_ref, side_ref, outs, joined = refs[:3], refs[3], refs[4], refs[5:9], refs[9]
    for head in range(HEADS):
        cols = pl.ds(head * HD, HD)
        table = packed_ref[:, GROUP:]
        other = (
            packed_ref[:, cols].astype(F32),
            undigit(table, head, 0, 3),
            undigit(table, head, 3, 2),
        )
        mixed, _, weight = blend([tuple(ref[:, cols] for ref in mine), other])
        joined[:, cols] = (mixed / weight + side_ref[:, cols]).astype(BF16)
    core, y_hi, z = here[0], here[3], here[4]
    step = 1 - 2 * core
    for out, shift in zip(outs, (0, step, -step, 2)):
        target = lax.rem(z + shift + 4, 4)
        for part in range(2):
            y = y_hi if part == 0 else 1 - y_hi
            start = pl.multiple_of(y * 256 + target * 64, 64)
            out[pl.ds(part * 64, 64), :] = joined[pl.ds(start, 64), :]


def join(here, mine, packed, side_part):
    return pl.pallas_call(
        join_body,
        out_shape=[jax.ShapeDtypeStruct((ROWS // 4, GROUP), BF16)] * 4,
        in_specs=[SMEM] + [VMEM] * 5,
        out_specs=[VMEM] * 4,
        scratch_shapes=[pltpu.VMEM((ROWS, GROUP), BF16)],
        compiler_params=PARAMS,
        cost_estimate=COST,
        name="join",
    )(here, *mine, packed, side_part)


def project_body(*refs):
    here, there, weights = refs[:4], refs[4:8], refs[8:12]
    keep, pair, core, both = refs[12:]
    width = keep.shape[1]
    left = [jnp.concatenate([here[i][...], there[j][...]], axis=0) for i, j in enumerate((0, 2, 1, 3))]
    tile = 512
    for start in range(0, width, tile):
        cols = pl.ds(start, tile)
        total = None
        for rows, w in zip(left, weights):
            part = lax.dot_general(rows, w[:, cols], NN, preferred_element_type=F32)
            total = part if total is None else total + part
        keep[:, cols] = total[:64]
        pair[:, cols] = total[64:128].astype(BF16)
        core[:, cols] = total[128:192].astype(BF16)
        both[:, cols] = total[192:].astype(BF16)


def project(here, there, weights):
    width = weights[0].shape[1]
    shape = lambda dtype: jax.ShapeDtypeStruct((64, width), dtype)
    return pl.pallas_call(
        project_body,
        out_shape=[shape(F32), shape(BF16), shape(BF16), shape(BF16)],
        compiler_params=PARAMS,
        cost_estimate=COST,
        name="project",
    )(*here, *there, *weights)


def total_body(here, keep, pair, core, both, out):
    width = keep.shape[1]
    mine = (keep[...] + pair[...].astype(F32)).astype(BF16)
    other = (core[...].astype(F32) + both[...].astype(F32)).astype(BF16)

    @pl.when(here[0] == 0)
    def _():
        out[:, :width] = mine
        out[:, width:] = other

    @pl.when(here[0] != 0)
    def _():
        out[:, :width] = other
        out[:, width:] = mine


def total(here, keep, pair, core, both):
    return pl.pallas_call(
        total_body,
        out_shape=jax.ShapeDtypeStruct((keep.shape[0], 2 * keep.shape[1]), BF16),
        in_specs=[SMEM] + [VMEM] * 4,
        out_specs=VMEM,
        compiler_params=PARAMS,
        cost_estimate=COST,
        name="total",
    )(here, keep, pair, core, both)


def on_device(
    video_q,
    video_k,
    video_v,
    audio_k,
    audio_v,
    text_k,
    text_v,
    block_start,
    block_len,
    prompt_len,
    w_out,
):
    seq = lax.axis_index("seq")
    aud = lax.axis_index("aud")
    here = jnp.stack([seq % 2, (seq // 2) % 4, seq // 8, aud // 4, aud % 4]).astype(jnp.int32)

    own = stage(here, video_k, video_v, text_k, text_v)
    own_c = send(own, CORE)
    kv1 = send(own, X_A)
    kv2 = send(own, X_B)
    asked = send(video_q, Y_LO)
    lent = send(lend(here, audio_k, audio_v), Y_NEAR)
    came = send(w_out, Z_A)
    (near_mine,) = flash("near_mine", [own, own_c], [video_q])
    (near_other,) = flash("near_other", [own, own_c], [asked])
    kv1, kv2, near_mine, near_other, lent = lax.optimization_barrier(
        (kv1, kv2, near_mine, near_other, lent)
    )
    dealt = deal(here, audio_k, audio_v, lent)
    audios = [dealt[0], send(dealt[1], Z_A), send(dealt[2], Z_B), send(dealt[3], Z_2)]
    kv3 = send(kv1, X_A)
    kv1_c = send(kv1, CORE)
    kv2_c = send(kv2, CORE)
    mid_mine, mid_other = flash("mid", [kv1, kv2, kv1_c, kv2_c], [after(video_q, came), asked])
    kv3, mid_mine, mid_other, *audios = lax.optimization_barrier(
        (kv3, mid_mine, mid_other, *audios)
    )
    kv3_c = send(kv3, CORE)
    text = prompt(own, kv1, kv2, kv3)
    text_y = send(text, Y_LO)
    (packed,) = flash(
        "far_other", [kv3, kv3_c], [asked], [[near_other, mid_other]], packed=True
    )
    packed, text_y = lax.optimization_barrier((packed, text_y))
    got = send(packed, Y_LO)
    w0, w1, w2 = split(here, w_out, after(came, packed))
    w3 = send(w1, Z_A)
    w2 = send(w2, CORE)
    text_yc = send(text_y, CORE)
    (far_mine,) = flash("far_mine", [kv3, kv3_c], [after(video_q, packed, w2)], [[near_mine, mid_mine]])
    side_part = side(
        here,
        block_start,
        block_len,
        prompt_len,
        after(video_q, packed),
        audios,
        [own, kv1, kv2, kv3, own_c, kv1_c, kv2_c, kv3_c],
        [text_y, text_yc],
    )

    parts = join(here, far_mine, got, side_part)
    mine = [parts[0], send(parts[1], Z_A), send(parts[2], Z_B), send(parts[3], Z_2)]
    theirs = [send(part, CORE) for part in mine]
    keep, pair, cross, both = project(mine, theirs, [w0, w1, w2, w3])
    pair = send(pair, Y_HI)
    both = send(both, Y_HI_CORE)
    cross = send(cross, CORE)
    return total(here, keep, pair, cross, both)


def solution(mesh):
    placed = (
        P("seq", "aud"),
        P("seq", "aud"),
        P("seq", "aud"),
        P("aud", None),
        P("aud", None),
        P("seq", "aud"),
        P("seq", "aud"),
        P("seq"),
        P("seq"),
        P(),
        P("aud", None),
    )
    return jax.shard_map(
        on_device, mesh=mesh, in_specs=placed, out_specs=P(("seq", "aud"), None), check_vma=False
    )
```

```python
import functools
import itertools

import jax
import jax.numpy as jnp
from jax import lax
from jax.experimental import pallas as pl
from jax.experimental.pallas import tpu as pltpu
from jax.sharding import PartitionSpec as P

HD = 128
HEADS = 3
GROUP = HEADS * HD
SUB = 256
DIGITS = 16
ROWS = 512
TEXT = 32
SCALE = HD ** (-0.5) * 1.4426950408889634
DEAD = -1e30
AXES = ("seq", "aud")
NT = (((1,), (1,)), ((), ()))
NN = (((1,), (0,)), ((), ()))
TN = (((0,), (0,)), ((), ()))
F32 = jnp.float32
BF16 = jnp.bfloat16
PARAMS = pltpu.CompilerParams(vmem_limit_bytes=20 * 2**20)
WIDE = pltpu.CompilerParams(vmem_limit_bytes=60 * 2**20)
COST = pl.CostEstimate(flops=1024, bytes_accessed=1024, transcendentals=0)


def lasting(us):
    return pl.CostEstimate(flops=int(us * 1.15e9), bytes_accessed=1024, transcendentals=0)


TIMES = dict(near_mine=2.4, near_other=2.4, mid=8.0, far_other=2.8, far_mine=26.0, side=20.0, join=20.0)
SMEM = pl.BlockSpec(memory_space=pltpu.SMEM)
VMEM = pl.BlockSpec(memory_space=pltpu.VMEM)
HBM = pl.BlockSpec(memory_space=pltpu.HBM)


def pairs(move):
    index = lambda yl, x, c, yh, z: ((yl * 4 + x) * 2 + c) * 8 + yh * 4 + z
    places = itertools.product(range(2), range(4), range(2), range(2), range(4))
    return [(index(*place), index(*move(*place))) for place in places]


X_A = pairs(lambda yl, x, c, yh, z: (yl, (x + 1 - 2 * c) % 4, c, yh, z))
X_B = pairs(lambda yl, x, c, yh, z: (yl, (x - 1 + 2 * c) % 4, c, yh, z))
Z_A = pairs(lambda yl, x, c, yh, z: (yl, x, c, yh, (z + 1 - 2 * c) % 4))
Z_B = pairs(lambda yl, x, c, yh, z: (yl, x, c, yh, (z - 1 + 2 * c) % 4))
Z_2 = pairs(lambda yl, x, c, yh, z: (yl, x, c, yh, (z + 2) % 4))
Y_LO = pairs(lambda yl, x, c, yh, z: (1 - yl, x, c, yh, z))
Y_NEAR = pairs(lambda yl, x, c, yh, z: (1 - yl, x, c, 1 - yh, z))
Y_HI = pairs(lambda yl, x, c, yh, z: (yl, x, c, 1 - yh, z))
CORE = pairs(lambda yl, x, c, yh, z: (yl, x, 1 - c, yh, z))
Y_HI_CORE = pairs(lambda yl, x, c, yh, z: (yl, x, 1 - c, 1 - yh, z))


def send(array, route):
    return lax.ppermute(array, AXES, route)


def after(value, *others):
    return lax.optimization_barrier((value,) + others)[0]


def with_ones(values):
    return jnp.concatenate([values, jnp.ones((values.shape[0], HD), BF16)], axis=1)


def move(sem, *pairs_of_refs):
    copies = [pltpu.make_async_copy(*pair, sem.at[i]) for i, pair in enumerate(pairs_of_refs)]
    for copy in copies:
        copy.start()
    for copy in copies:
        copy.wait()


def stage_body(_, k, v, tk, tv, own, sem):
    left, right = pl.ds(0, GROUP), pl.ds(GROUP, GROUP)
    above, below = pl.ds(0, ROWS), pl.ds(ROWS, TEXT)
    move(
        sem,
        (k, own.at[above, left]),
        (v, own.at[above, right]),
        (tk, own.at[below, left]),
        (tv, own.at[below, right]),
    )


def stage(*parts):
    return pl.pallas_call(
        stage_body,
        out_shape=jax.ShapeDtypeStruct((ROWS + TEXT, 2 * GROUP), BF16),
        in_specs=[SMEM] + [HBM] * 4,
        out_specs=VMEM,
        scratch_shapes=[pltpu.SemaphoreType.DMA((4,))],
        compiler_params=WIDE,
        cost_estimate=COST,
        name="stage",
    )(*parts)


def split_body(here, w, came, own, keep, give):
    width = own.shape[1]
    half = pl.ds(pl.multiple_of(here[0] * width, width), width)
    rest = pl.ds(pl.multiple_of((1 - here[0]) * width, width), width)
    own[...] = w[:, half]
    keep[...] = came[:, half]
    give[...] = came[:, rest]


def split(here, w, came):
    half = jax.ShapeDtypeStruct((w.shape[0], w.shape[1] // 2), BF16)
    return pl.pallas_call(
        split_body,
        out_shape=[half] * 3,
        in_specs=[SMEM, VMEM, VMEM],
        out_specs=[VMEM] * 3,
        compiler_params=PARAMS,
        cost_estimate=COST,
        name="split",
    )(here, w, came)


def lend_body(here, ak, av, out, sem):
    width = out.shape[1]
    rows = ak.shape[0]
    cols = pl.ds(pl.multiple_of((1 - here[3]) * width, width), width)
    move(sem, (ak.at[:, cols], out.at[pl.ds(0, rows)]), (av.at[:, cols], out.at[pl.ds(rows, rows)]))


def lend(here, ak, av):
    return pl.pallas_call(
        lend_body,
        out_shape=jax.ShapeDtypeStruct((2 * ak.shape[0], ak.shape[1] // 2), BF16),
        in_specs=[SMEM, HBM, HBM],
        out_specs=VMEM,
        scratch_shapes=[pltpu.SemaphoreType.DMA((2,))],
        compiler_params=PARAMS,
        cost_estimate=COST,
        name="lend",
    )(here, ak, av)


def prompt_body(*refs):
    for number, ref in enumerate(refs[:-1]):
        refs[-1][pl.ds(number * TEXT, TEXT), :] = ref[...]


BELOW = pl.BlockSpec((TEXT, 2 * GROUP), lambda i: (ROWS // TEXT, 0))


def prompt(*arrays):
    return pl.pallas_call(
        prompt_body,
        out_shape=jax.ShapeDtypeStruct((len(arrays) * TEXT, 2 * GROUP), BF16),
        grid=(1,),
        in_specs=[BELOW] * len(arrays),
        out_specs=VMEM,
        compiler_params=PARAMS,
        cost_estimate=COST,
        name="prompt",
    )(*arrays)


def deal_body(here, ak, av, lent, *outs):
    core, y_hi, z = here[0], here[3], here[4]
    rows = ak.shape[0]
    step = 1 - 2 * core
    for out, shift in zip(outs, (0, step, -step, 2)):
        target = lax.rem(z + shift + 4, 4)
        cols = pl.ds(pl.multiple_of((y_hi * 4 + target) * GROUP, GROUP), GROUP)
        out[:rows, :] = ak[:, cols]
        out[rows : 2 * rows, :] = av[:, cols]
        out[2 * rows :, :] = lent[:, pl.ds(pl.multiple_of(target * GROUP, GROUP), GROUP)]


def deal(here, ak, av, lent):
    return pl.pallas_call(
        deal_body,
        out_shape=[jax.ShapeDtypeStruct((4 * ak.shape[0], GROUP), BF16)] * 4,
        in_specs=[SMEM, VMEM, VMEM, VMEM],
        out_specs=[VMEM] * 4,
        compiler_params=PARAMS,
        cost_estimate=COST,
        name="deal",
    )(here, ak, av, lent)


def digits(column, count):
    out = []
    for _ in range(count):
        digit = column.astype(BF16).astype(F32)
        column = column - digit
        out.append(digit)
    return out


def undigit(table, head, first, count):
    row = lax.broadcasted_iota(jnp.int32, (DIGITS, HD), 0)
    picked = (row % HEADS == head) & (row >= first * HEADS) & (row < (first + count) * HEADS)
    picked = picked.astype(F32).astype(BF16)
    return lax.dot_general(table, picked, TN, preferred_element_type=F32)


def blend(parts):
    peak = functools.reduce(jnp.maximum, [part[1] for part in parts])
    scales = [jnp.exp2(part[1] - peak) for part in parts]
    mixed = functools.reduce(lambda a, b: a + b, [p[0] * w for p, w in zip(parts, scales)])
    weight = functools.reduce(lambda a, b: a + b, [p[2] * w for p, w in zip(parts, scales)])
    return mixed, peak, weight


def flash_body(n_arrays, n_sets, n_priors, packed, *refs):
    arrays = refs[:n_arrays]
    queries = refs[n_arrays : n_arrays + n_sets]
    refs = refs[n_arrays + n_sets :]
    priors = refs[: 3 * n_sets * n_priors]
    outs = refs[3 * n_sets * n_priors :]
    lane = lax.broadcasted_iota(jnp.int32, (SUB, HD), 1)
    for number in range(n_sets):
        for start in range(0, ROWS, SUB):
            rows = pl.ds(start, SUB)
            table = jnp.zeros((SUB, HD), F32)
            for head in range(HEADS):
                cols = pl.ds(head * HD, HD)
                vcols = pl.ds(GROUP + head * HD, HD)
                q = queries[number][rows, cols]
                scores = []
                peak = None
                for array in arrays:
                    s = lax.dot_general(q, array[:ROWS, cols], NT, preferred_element_type=F32) * SCALE
                    scores.append(s)
                    top = jnp.max(s, axis=1, keepdims=True)
                    peak = top if peak is None else jnp.maximum(peak, top)
                total = None
                for s, array in zip(scores, arrays):
                    p = jnp.exp2(s - peak).astype(BF16)
                    v = with_ones(array[:ROWS, vcols])
                    part = lax.dot_general(p, v, NN, preferred_element_type=F32)
                    total = part if total is None else total + part
                result = (total[:, :HD], jnp.broadcast_to(peak, (SUB, HD)), total[:, HD:])
                if n_priors:
                    parts = [result]
                    for i in range(n_priors):
                        at = 3 * (number * n_priors + i)
                        parts.append(tuple(priors[at + j][rows, cols] for j in range(3)))
                    result = blend(parts)
                if packed:
                    outs[number][rows, cols] = result[0].astype(BF16)
                    for piece, digit in enumerate(digits(result[1], 3) + digits(result[2], 2)):
                        table = jnp.where(lane == piece * HEADS + head, digit, table)
                else:
                    for j in range(3):
                        outs[3 * number + j][rows, cols] = result[j]
            if packed:
                below = pl.ds(ROWS + start // SUB * DIGITS, DIGITS)
                outs[number][below, :SUB] = jnp.transpose(table)[:DIGITS].astype(BF16)
                outs[number][below, SUB:] = jnp.zeros((DIGITS, GROUP - SUB), BF16)


def flash(name, arrays, queries, priors=None, packed=False):
    n_sets, n_arrays = len(queries), len(arrays)
    priors = priors or [[] for _ in queries]
    n_priors = len(priors[0])
    flat = [ref for parts in priors for part in parts for ref in part]
    if packed:
        shapes = [jax.ShapeDtypeStruct((ROWS + ROWS // SUB * DIGITS, GROUP), BF16)] * n_sets
    else:
        shapes = [jax.ShapeDtypeStruct((ROWS, GROUP), F32)] * (3 * n_sets)
    outs = pl.pallas_call(
        functools.partial(flash_body, n_arrays, n_sets, n_priors, packed),
        out_shape=shapes,
        compiler_params=PARAMS,
        cost_estimate=lasting(TIMES[name]),
        name=name,
    )(*arrays, *queries, *flat)
    return outs if packed else [tuple(outs[3 * i : 3 * i + 3]) for i in range(n_sets)]


def side_body(here, start_ref, length_ref, prompt_ref, q_ref, *refs):
    audios, texts, out_ref = refs[:4], refs[4:14], refs[14]
    core, x, y_lo, y_hi, z = [here[i] for i in range(5)]
    lane = lax.broadcasted_iota(jnp.int32, (1, 16 * TEXT), 1)
    place = jnp.zeros((1, 16 * TEXT), jnp.int32)
    for number in range(16):
        y = y_lo if number < 8 else 1 - y_lo
        c = core if number % 8 < 4 else 1 - core
        step = 2 * c - 1
        shift = (0, step, -step, 2)[number % 4]
        block = y * 8 + lax.rem(x + shift + 4, 4) * 2 + c
        place = jnp.where(lane // TEXT == number, block * TEXT + lane % TEXT, place)
    live = place < prompt_ref[0]
    shard = audios[0].shape[0] // 4
    heard_at = jnp.zeros((1, 8 * shard), jnp.int32)
    lane = lax.broadcasted_iota(jnp.int32, (1, 8 * shard), 1)
    step = 1 - 2 * core
    for number in range(8):
        source = lax.rem(z + (0, -step, step, 2)[number // 2] + 4, 4)
        y = y_hi if number % 2 == 0 else 1 - y_hi
        block = y * 4 + source
        heard_at = jnp.where(lane // shard == number, block * shard + lane % shard, heard_at)
    for head in range(HEADS):
        cols = pl.ds(head * HD, HD)
        vcols = pl.ds(GROUP + head * HD, HD)
        text_k = jnp.concatenate([ref[:, cols] for ref in texts], axis=0)
        text_v = with_ones(jnp.concatenate([ref[:, vcols] for ref in texts], axis=0))
        parts = [(ref, half) for ref in audios for half in (0, 2 * shard)]
        audio_k = jnp.concatenate([ref[pl.ds(half, shard), cols] for ref, half in parts], axis=0)
        audio_v = [ref[pl.ds(half + shard, shard), cols] for ref, half in parts]
        audio_v = with_ones(jnp.concatenate(audio_v, axis=0))
        for block in range(ROWS // HD):
            rows = pl.ds(block * HD, HD)
            q = q_ref[rows, cols]
            s = lax.dot_general(q, text_k, NT, preferred_element_type=F32) * SCALE
            s = jnp.where(live, s, DEAD)
            p = jnp.exp2(s - jnp.max(s, axis=1, keepdims=True)).astype(BF16)
            mix = lax.dot_general(p, text_v, NN, preferred_element_type=F32)
            s = lax.dot_general(q, audio_k, NT, preferred_element_type=F32) * SCALE
            begin = start_ref[block]
            inside = (heard_at >= begin) & (heard_at < begin + length_ref[block])
            s = jnp.where(inside, s, DEAD)
            p = jnp.exp2(s - jnp.max(s, axis=1, keepdims=True)).astype(BF16)
            heard = lax.dot_general(p, audio_v, NN, preferred_element_type=F32)
            out_ref[rows, cols] = heard[:, :HD] / heard[:, HD:] + mix[:, :HD] / mix[:, HD:]


def side(here, block_start, block_len, prompt_len, q, audios, texts, pair_texts):
    return pl.pallas_call(
        side_body,
        out_shape=jax.ShapeDtypeStruct(q.shape, F32),
        grid=(1,),
        in_specs=[SMEM] * 4 + [VMEM] * 5 + [BELOW] * 8 + [VMEM] * 2,
        out_specs=VMEM,
        compiler_params=PARAMS,
        cost_estimate=lasting(TIMES["side"]),
        name="side",
    )(here, block_start, block_len, prompt_len, q, *audios, *texts, *pair_texts)


def join_body(here, *refs):
    mine, packed_ref, side_ref, outs, joined = refs[:3], refs[3], refs[4], refs[5:9], refs[9]
    for start in range(0, ROWS, SUB):
        rows = pl.ds(start, SUB)
        table = packed_ref[pl.ds(ROWS + start // SUB * DIGITS, DIGITS), :SUB]
        for head in range(HEADS):
            cols = pl.ds(head * HD, HD)
            other = (
                packed_ref[rows, cols].astype(F32),
                undigit(table, head, 0, 3),
                undigit(table, head, 3, 2),
            )
            mixed, _, weight = blend([tuple(ref[rows, cols] for ref in mine), other])
            joined[rows, cols] = (mixed / weight + side_ref[rows, cols]).astype(BF16)
    core, y_hi, z = here[0], here[3], here[4]
    step = 1 - 2 * core
    for out, shift in zip(outs, (0, step, -step, 2)):
        target = lax.rem(z + shift + 4, 4)
        for part in range(2):
            y = y_hi if part == 0 else 1 - y_hi
            start = pl.multiple_of(y * 256 + target * 64, 64)
            out[pl.ds(part * 64, 64), :] = joined[pl.ds(start, 64), :]


def join(here, mine, packed, side_part):
    return pl.pallas_call(
        join_body,
        out_shape=[jax.ShapeDtypeStruct((ROWS // 4, GROUP), BF16)] * 4,
        in_specs=[SMEM] + [VMEM] * 5,
        out_specs=[VMEM] * 4,
        scratch_shapes=[pltpu.VMEM((ROWS, GROUP), BF16)],
        compiler_params=PARAMS,
        cost_estimate=lasting(TIMES["join"]),
        name="join",
    )(here, *mine, packed, side_part)


def project_body(*refs):
    here, there, weights = refs[:4], refs[4:8], refs[8:12]
    keep, pair, core, both = refs[12:]
    width = keep.shape[1]
    left = [jnp.concatenate([here[i][...], there[j][...]], axis=0) for i, j in enumerate((0, 2, 1, 3))]
    tile = 512
    for start in range(0, width, tile):
        cols = pl.ds(start, tile)
        total = None
        for rows, w in zip(left, weights):
            part = lax.dot_general(rows, w[:, cols], NN, preferred_element_type=F32)
            total = part if total is None else total + part
        keep[:, cols] = total[:64]
        pair[:, cols] = total[64:128].astype(BF16)
        core[:, cols] = total[128:192].astype(BF16)
        both[:, cols] = total[192:].astype(BF16)


def project(here, there, weights):
    width = weights[0].shape[1]
    shape = lambda dtype: jax.ShapeDtypeStruct((64, width), dtype)
    return pl.pallas_call(
        project_body,
        out_shape=[shape(F32), shape(BF16), shape(BF16), shape(BF16)],
        compiler_params=PARAMS,
        cost_estimate=COST,
        name="project",
    )(*here, *there, *weights)


def total_body(here, keep, pair, core, both, out):
    width = keep.shape[1]
    mine = (keep[...] + pair[...].astype(F32)).astype(BF16)
    other = (core[...].astype(F32) + both[...].astype(F32)).astype(BF16)

    @pl.when(here[0] == 0)
    def _():
        out[:, :width] = mine
        out[:, width:] = other

    @pl.when(here[0] != 0)
    def _():
        out[:, :width] = other
        out[:, width:] = mine


def total(here, keep, pair, core, both):
    return pl.pallas_call(
        total_body,
        out_shape=jax.ShapeDtypeStruct((keep.shape[0], 2 * keep.shape[1]), BF16),
        in_specs=[SMEM] + [VMEM] * 4,
        out_specs=VMEM,
        compiler_params=PARAMS,
        cost_estimate=COST,
        name="total",
    )(here, keep, pair, core, both)


def on_device(
    video_q,
    video_k,
    video_v,
    audio_k,
    audio_v,
    text_k,
    text_v,
    block_start,
    block_len,
    prompt_len,
    w_out,
):
    seq = lax.axis_index("seq")
    aud = lax.axis_index("aud")
    here = jnp.stack([seq % 2, (seq // 2) % 4, seq // 8, aud // 4, aud % 4]).astype(jnp.int32)

    own = stage(here, video_k, video_v, text_k, text_v)
    own_c = send(own, CORE)
    kv1 = send(own, X_A)
    kv2 = send(own, X_B)
    asked = send(video_q, Y_LO)
    lent = send(lend(here, audio_k, audio_v), Y_NEAR)
    came = send(w_out, Z_A)
    (near_mine,) = flash("near_mine", [own, own_c], [video_q])
    (near_other,) = flash("near_other", [own, own_c], [asked])
    kv1, kv2, near_mine, near_other, lent = lax.optimization_barrier(
        (kv1, kv2, near_mine, near_other, lent)
    )
    dealt = deal(here, audio_k, audio_v, lent)
    audios = [dealt[0], send(dealt[1], Z_A), send(dealt[2], Z_B), send(dealt[3], Z_2)]
    kv3 = send(kv1, X_A)
    kv1_c = send(kv1, CORE)
    kv2_c = send(kv2, CORE)
    mid_mine, mid_other = flash("mid", [kv1, kv2, kv1_c, kv2_c], [after(video_q, came), asked])
    kv3, mid_mine, mid_other, *audios = lax.optimization_barrier(
        (kv3, mid_mine, mid_other, *audios)
    )
    kv3_c = send(kv3, CORE)
    w0, w1, w2 = split(here, w_out, after(came, *mid_mine))
    w3 = send(w1, Z_A)
    w2 = send(w2, CORE)
    text = prompt(own, kv1, kv2, kv3)
    text_y = send(text, Y_LO)
    (packed,) = flash(
        "far_other", [kv3, kv3_c], [after(asked, w0)], [[near_other, mid_other]], packed=True
    )
    got = send(packed, Y_LO)
    text_y = after(text_y, packed)
    text_yc = send(text_y, CORE)
    (far_mine,) = flash("far_mine", [kv3, kv3_c], [after(video_q, packed)], [[near_mine, mid_mine]])
    side_part = side(
        here,
        block_start,
        block_len,
        prompt_len,
        after(video_q, packed),
        audios,
        [own, kv1, kv2, kv3, own_c, kv1_c, kv2_c, kv3_c],
        [text_y, text_yc],
    )

    parts = join(here, far_mine, got, side_part)
    mine = [parts[0], send(parts[1], Z_A), send(parts[2], Z_B), send(parts[3], Z_2)]
    theirs = [send(part, CORE) for part in mine]
    keep, pair, cross, both = project(mine, theirs, [w0, w1, w2, w3])
    pair = send(pair, Y_HI)
    both = send(both, Y_HI_CORE)
    cross = send(cross, CORE)
    return total(here, keep, pair, cross, both)


def solution(mesh):
    placed = (
        P("seq", "aud"),
        P("seq", "aud"),
        P("seq", "aud"),
        P("aud", None),
        P("aud", None),
        P("seq", "aud"),
        P("seq", "aud"),
        P("seq"),
        P("seq"),
        P(),
        P("aud", None),
    )
    return jax.shard_map(
        on_device, mesh=mesh, in_specs=placed, out_specs=P(("seq", "aud"), None), check_vma=False
    )
```

```python
import functools
import itertools

import jax
import jax.numpy as jnp
from jax import lax
from jax.experimental import pallas as pl
from jax.experimental.pallas import tpu as pltpu
from jax.sharding import PartitionSpec as P

HD = 128
HEADS = 3
GROUP = HEADS * HD
SUB = 256
DIGITS = 16
ROWS = 512
TEXT = 32
SCALE = HD ** (-0.5) * 1.4426950408889634
DEAD = -1e30
AXES = ("seq", "aud")
NT = (((1,), (1,)), ((), ()))
NN = (((1,), (0,)), ((), ()))
TN = (((0,), (0,)), ((), ()))
F32 = jnp.float32
BF16 = jnp.bfloat16
PARAMS = pltpu.CompilerParams(vmem_limit_bytes=20 * 2**20)
WIDE = pltpu.CompilerParams(vmem_limit_bytes=60 * 2**20)
COST = pl.CostEstimate(flops=1024, bytes_accessed=1024, transcendentals=0)


def lasting(us):
    return pl.CostEstimate(flops=int(us * 1.15e9), bytes_accessed=1024, transcendentals=0)


TIMES = dict(near_mine=2.4, near_other=2.4, mid=8.0, far_other=2.8, far_mine=26.0, side=2.7, join=20.0)
SMEM = pl.BlockSpec(memory_space=pltpu.SMEM)
VMEM = pl.BlockSpec(memory_space=pltpu.VMEM)
HBM = pl.BlockSpec(memory_space=pltpu.HBM)


def pairs(move):
    index = lambda yl, x, c, yh, z: ((yl * 4 + x) * 2 + c) * 8 + yh * 4 + z
    places = itertools.product(range(2), range(4), range(2), range(2), range(4))
    return [(index(*place), index(*move(*place))) for place in places]


X_A = pairs(lambda yl, x, c, yh, z: (yl, (x + 1 - 2 * c) % 4, c, yh, z))
X_B = pairs(lambda yl, x, c, yh, z: (yl, (x - 1 + 2 * c) % 4, c, yh, z))
Z_A = pairs(lambda yl, x, c, yh, z: (yl, x, c, yh, (z + 1 - 2 * c) % 4))
Z_B = pairs(lambda yl, x, c, yh, z: (yl, x, c, yh, (z - 1 + 2 * c) % 4))
Z_2 = pairs(lambda yl, x, c, yh, z: (yl, x, c, yh, (z + 2) % 4))
Y_LO = pairs(lambda yl, x, c, yh, z: (1 - yl, x, c, yh, z))
Y_NEAR = pairs(lambda yl, x, c, yh, z: (1 - yl, x, c, 1 - yh, z))
Y_HI = pairs(lambda yl, x, c, yh, z: (yl, x, c, 1 - yh, z))
CORE = pairs(lambda yl, x, c, yh, z: (yl, x, 1 - c, yh, z))
Y_HI_CORE = pairs(lambda yl, x, c, yh, z: (yl, x, 1 - c, 1 - yh, z))


def send(array, route):
    return lax.ppermute(array, AXES, route)


def after(value, *others):
    return lax.optimization_barrier((value,) + others)[0]


def with_ones(values):
    return jnp.concatenate([values, jnp.ones((values.shape[0], HD), BF16)], axis=1)


def move(sem, *pairs_of_refs):
    copies = [pltpu.make_async_copy(*pair, sem.at[i]) for i, pair in enumerate(pairs_of_refs)]
    for copy in copies:
        copy.start()
    for copy in copies:
        copy.wait()


def stage_body(_, k, v, tk, tv, own, sem):
    left, right = pl.ds(0, GROUP), pl.ds(GROUP, GROUP)
    above, below = pl.ds(0, ROWS), pl.ds(ROWS, TEXT)
    move(
        sem,
        (k, own.at[above, left]),
        (v, own.at[above, right]),
        (tk, own.at[below, left]),
        (tv, own.at[below, right]),
    )


def stage(*parts):
    return pl.pallas_call(
        stage_body,
        out_shape=jax.ShapeDtypeStruct((ROWS + TEXT, 2 * GROUP), BF16),
        in_specs=[SMEM] + [HBM] * 4,
        out_specs=VMEM,
        scratch_shapes=[pltpu.SemaphoreType.DMA((4,))],
        compiler_params=WIDE,
        cost_estimate=COST,
        name="stage",
    )(*parts)


def split_body(here, w, came, own, keep, give):
    width = own.shape[1]
    half = pl.ds(pl.multiple_of(here[0] * width, width), width)
    rest = pl.ds(pl.multiple_of((1 - here[0]) * width, width), width)
    own[...] = w[:, half]
    keep[...] = came[:, half]
    give[...] = came[:, rest]


def split(here, w, came):
    half = jax.ShapeDtypeStruct((w.shape[0], w.shape[1] // 2), BF16)
    return pl.pallas_call(
        split_body,
        out_shape=[half] * 3,
        in_specs=[SMEM, VMEM, VMEM],
        out_specs=[VMEM] * 3,
        compiler_params=PARAMS,
        cost_estimate=COST,
        name="split",
    )(here, w, came)


def lend_body(here, ak, av, out):
    cols = pl.ds(pl.multiple_of((1 - here[3]) * out.shape[1], out.shape[1]), out.shape[1])
    out[...] = jnp.where(here[0] == 0, ak[:, cols], av[:, cols])


def lend(here, ak, av):
    return pl.pallas_call(
        lend_body,
        out_shape=jax.ShapeDtypeStruct((ak.shape[0], ak.shape[1] // 2), BF16),
        in_specs=[SMEM, VMEM, VMEM],
        out_specs=VMEM,
        compiler_params=PARAMS,
        cost_estimate=COST,
        name="lend",
    )(here, ak, av)


def prompt_body(*refs):
    for number, ref in enumerate(refs[:-1]):
        refs[-1][pl.ds(number * TEXT, TEXT), :] = ref[...]


BELOW = pl.BlockSpec((TEXT, 2 * GROUP), lambda i: (ROWS // TEXT, 0))


def prompt(*arrays):
    return pl.pallas_call(
        prompt_body,
        out_shape=jax.ShapeDtypeStruct((len(arrays) * TEXT, 2 * GROUP), BF16),
        grid=(1,),
        in_specs=[BELOW] * len(arrays),
        out_specs=VMEM,
        compiler_params=PARAMS,
        cost_estimate=COST,
        name="prompt",
    )(*arrays)


def deal_body(here, ak, av, lent, *outs):
    core, y_hi, z = here[0], here[3], here[4]
    rows = ak.shape[0]
    step = 1 - 2 * core
    for out, shift in zip(outs, (0, step, -step, 2)):
        target = lax.rem(z + shift + 4, 4)
        cols = pl.ds(pl.multiple_of((y_hi * 4 + target) * GROUP, GROUP), GROUP)
        out[:rows, :] = jnp.where(core == 0, ak[:, cols], av[:, cols])
        out[rows:, :] = lent[:, pl.ds(pl.multiple_of(target * GROUP, GROUP), GROUP)]


def deal(here, ak, av, lent):
    return pl.pallas_call(
        deal_body,
        out_shape=[jax.ShapeDtypeStruct((2 * ak.shape[0], GROUP), BF16)] * 4,
        in_specs=[SMEM, VMEM, VMEM, VMEM],
        out_specs=[VMEM] * 4,
        compiler_params=PARAMS,
        cost_estimate=COST,
        name="deal",
    )(here, ak, av, lent)


def digits(column, count):
    out = []
    for _ in range(count):
        digit = column.astype(BF16).astype(F32)
        column = column - digit
        out.append(digit)
    return out


def undigit(table, head, first, count):
    row = lax.broadcasted_iota(jnp.int32, (DIGITS, HD), 0)
    picked = (row % HEADS == head) & (row >= first * HEADS) & (row < (first + count) * HEADS)
    picked = picked.astype(F32).astype(BF16)
    return lax.dot_general(table, picked, TN, preferred_element_type=F32)


def blend(parts):
    peak = functools.reduce(jnp.maximum, [part[1] for part in parts])
    scales = [jnp.exp2(part[1] - peak) for part in parts]
    mixed = functools.reduce(lambda a, b: a + b, [p[0] * w for p, w in zip(parts, scales)])
    weight = functools.reduce(lambda a, b: a + b, [p[2] * w for p, w in zip(parts, scales)])
    return mixed, peak, weight


def flash_body(n_arrays, n_sets, n_priors, packed, *refs):
    arrays = refs[:n_arrays]
    queries = refs[n_arrays : n_arrays + n_sets]
    refs = refs[n_arrays + n_sets :]
    priors = refs[: 3 * n_sets * n_priors]
    outs = refs[3 * n_sets * n_priors :]
    lane = lax.broadcasted_iota(jnp.int32, (SUB, HD), 1)
    for number in range(n_sets):
        for start in range(0, ROWS, SUB):
            rows = pl.ds(start, SUB)
            table = jnp.zeros((SUB, HD), F32)
            for head in range(HEADS):
                cols = pl.ds(head * HD, HD)
                vcols = pl.ds(GROUP + head * HD, HD)
                q = queries[number][rows, cols]
                scores = []
                peak = None
                for array in arrays:
                    s = lax.dot_general(q, array[:ROWS, cols], NT, preferred_element_type=F32) * SCALE
                    scores.append(s)
                    top = jnp.max(s, axis=1, keepdims=True)
                    peak = top if peak is None else jnp.maximum(peak, top)
                total = None
                for s, array in zip(scores, arrays):
                    p = jnp.exp2(s - peak).astype(BF16)
                    v = with_ones(array[:ROWS, vcols])
                    part = lax.dot_general(p, v, NN, preferred_element_type=F32)
                    total = part if total is None else total + part
                result = (total[:, :HD], jnp.broadcast_to(peak, (SUB, HD)), total[:, HD:])
                if n_priors:
                    parts = [result]
                    for i in range(n_priors):
                        at = 3 * (number * n_priors + i)
                        parts.append(tuple(priors[at + j][rows, cols] for j in range(3)))
                    result = blend(parts)
                if packed:
                    outs[number][rows, cols] = result[0].astype(BF16)
                    for piece, digit in enumerate(digits(result[1], 3) + digits(result[2], 2)):
                        table = jnp.where(lane == piece * HEADS + head, digit, table)
                else:
                    for j in range(3):
                        outs[3 * number + j][rows, cols] = result[j]
            if packed:
                below = pl.ds(ROWS + start // SUB * DIGITS, DIGITS)
                outs[number][below, :SUB] = jnp.transpose(table)[:DIGITS].astype(BF16)
                outs[number][below, SUB:] = jnp.zeros((DIGITS, GROUP - SUB), BF16)


def flash(name, arrays, queries, priors=None, packed=False):
    n_sets, n_arrays = len(queries), len(arrays)
    priors = priors or [[] for _ in queries]
    n_priors = len(priors[0])
    flat = [ref for parts in priors for part in parts for ref in part]
    if packed:
        shapes = [jax.ShapeDtypeStruct((ROWS + ROWS // SUB * DIGITS, GROUP), BF16)] * n_sets
    else:
        shapes = [jax.ShapeDtypeStruct((ROWS, GROUP), F32)] * (3 * n_sets)
    outs = pl.pallas_call(
        functools.partial(flash_body, n_arrays, n_sets, n_priors, packed),
        out_shape=shapes,
        compiler_params=PARAMS,
        cost_estimate=lasting(TIMES[name]),
        name=name,
    )(*arrays, *queries, *flat)
    return outs if packed else [tuple(outs[3 * i : 3 * i + 3]) for i in range(n_sets)]


def side_body(here, start_ref, length_ref, prompt_ref, q_ref, *refs):
    mine, theirs, texts, out_ref = refs[:4], refs[4:8], refs[8:18], refs[18]
    core, x, y_lo, y_hi, z = [here[i] for i in range(5)]
    lane = lax.broadcasted_iota(jnp.int32, (1, 16 * TEXT), 1)
    place = jnp.zeros((1, 16 * TEXT), jnp.int32)
    for number in range(16):
        y = y_lo if number < 8 else 1 - y_lo
        c = core if number % 8 < 4 else 1 - core
        step = 2 * c - 1
        shift = (0, step, -step, 2)[number % 4]
        block = y * 8 + lax.rem(x + shift + 4, 4) * 2 + c
        place = jnp.where(lane // TEXT == number, block * TEXT + lane % TEXT, place)
    live = place < prompt_ref[0]
    shard = mine[0].shape[0] // 2
    heard_at = jnp.zeros((1, 8 * shard), jnp.int32)
    lane = lax.broadcasted_iota(jnp.int32, (1, 8 * shard), 1)
    for number in range(8):
        source = lax.rem(z + (0, 3, 1, 2)[number // 2], 4)
        y = y_hi if number % 2 == 0 else 1 - y_hi
        block = y * 4 + source
        heard_at = jnp.where(lane // shard == number, block * shard + lane % shard, heard_at)
    for head in range(HEADS):
        cols = pl.ds(head * HD, HD)
        vcols = pl.ds(GROUP + head * HD, HD)
        text_k = jnp.concatenate([ref[:, cols] for ref in texts], axis=0)
        text_v = with_ones(jnp.concatenate([ref[:, vcols] for ref in texts], axis=0))
        pick = lambda refs, order: jnp.concatenate([refs[i][:, cols] for i in order], axis=0)
        first, second = (0, 1, 2, 3), (0, 2, 1, 3)
        audio_k = jnp.where(core == 0, pick(mine, first), pick(theirs, first))
        audio_v = with_ones(jnp.where(core == 0, pick(theirs, second), pick(mine, second)))
        for block in range(ROWS // HD):
            rows = pl.ds(block * HD, HD)
            q = q_ref[rows, cols]
            s = lax.dot_general(q, text_k, NT, preferred_element_type=F32) * SCALE
            s = jnp.where(live, s, DEAD)
            p = jnp.exp2(s - jnp.max(s, axis=1, keepdims=True)).astype(BF16)
            mix = lax.dot_general(p, text_v, NN, preferred_element_type=F32)
            s = lax.dot_general(q, audio_k, NT, preferred_element_type=F32) * SCALE
            begin = start_ref[block]
            inside = (heard_at >= begin) & (heard_at < begin + length_ref[block])
            s = jnp.where(inside, s, DEAD)
            p = jnp.exp2(s - jnp.max(s, axis=1, keepdims=True)).astype(BF16)
            heard = lax.dot_general(p, audio_v, NN, preferred_element_type=F32)
            out_ref[rows, cols] = heard[:, :HD] / heard[:, HD:] + mix[:, :HD] / mix[:, HD:]


def side(here, block_start, block_len, prompt_len, q, audios, texts, pair_texts):
    return pl.pallas_call(
        side_body,
        out_shape=jax.ShapeDtypeStruct(q.shape, F32),
        grid=(1,),
        in_specs=[SMEM] * 4 + [VMEM] * 9 + [BELOW] * 8 + [VMEM] * 2,
        out_specs=VMEM,
        compiler_params=PARAMS,
        cost_estimate=lasting(TIMES["side"]),
        name="side",
    )(here, block_start, block_len, prompt_len, q, *audios, *texts, *pair_texts)


def join_body(here, *refs):
    mine, packed_ref, side_ref, outs, joined = refs[:3], refs[3], refs[4], refs[5:9], refs[9]
    for start in range(0, ROWS, SUB):
        rows = pl.ds(start, SUB)
        table = packed_ref[pl.ds(ROWS + start // SUB * DIGITS, DIGITS), :SUB]
        for head in range(HEADS):
            cols = pl.ds(head * HD, HD)
            other = (
                packed_ref[rows, cols].astype(F32),
                undigit(table, head, 0, 3),
                undigit(table, head, 3, 2),
            )
            mixed, _, weight = blend([tuple(ref[rows, cols] for ref in mine), other])
            joined[rows, cols] = (mixed / weight + side_ref[rows, cols]).astype(BF16)
    core, y_hi, z = here[0], here[3], here[4]
    step = 1 - 2 * core
    for out, shift in zip(outs, (0, step, -step, 2)):
        target = lax.rem(z + shift + 4, 4)
        for part in range(2):
            y = y_hi if part == 0 else 1 - y_hi
            start = pl.multiple_of(y * 256 + target * 64, 64)
            out[pl.ds(part * 64, 64), :] = joined[pl.ds(start, 64), :]


def join(here, mine, packed, side_part):
    return pl.pallas_call(
        join_body,
        out_shape=[jax.ShapeDtypeStruct((ROWS // 4, GROUP), BF16)] * 4,
        in_specs=[SMEM] + [VMEM] * 5,
        out_specs=[VMEM] * 4,
        scratch_shapes=[pltpu.VMEM((ROWS, GROUP), BF16)],
        compiler_params=PARAMS,
        cost_estimate=lasting(TIMES["join"]),
        name="join",
    )(here, *mine, packed, side_part)


def project_body(*refs):
    here, there, weights = refs[:4], refs[4:8], refs[8:12]
    keep, pair, core, both = refs[12:]
    width = keep.shape[1]
    left = [jnp.concatenate([here[i][...], there[j][...]], axis=0) for i, j in enumerate((0, 2, 1, 3))]
    tile = 512
    for start in range(0, width, tile):
        cols = pl.ds(start, tile)
        total = None
        for rows, w in zip(left, weights):
            part = lax.dot_general(rows, w[:, cols], NN, preferred_element_type=F32)
            total = part if total is None else total + part
        keep[:, cols] = total[:64]
        pair[:, cols] = total[64:128].astype(BF16)
        core[:, cols] = total[128:192].astype(BF16)
        both[:, cols] = total[192:].astype(BF16)


def project(here, there, weights):
    width = weights[0].shape[1]
    shape = lambda dtype: jax.ShapeDtypeStruct((64, width), dtype)
    return pl.pallas_call(
        project_body,
        out_shape=[shape(F32), shape(BF16), shape(BF16), shape(BF16)],
        compiler_params=PARAMS,
        cost_estimate=COST,
        name="project",
    )(*here, *there, *weights)


def total_body(here, keep, pair, core, both, out):
    width = keep.shape[1]
    mine = (keep[...] + pair[...].astype(F32)).astype(BF16)
    other = (core[...].astype(F32) + both[...].astype(F32)).astype(BF16)

    @pl.when(here[0] == 0)
    def _():
        out[:, :width] = mine
        out[:, width:] = other

    @pl.when(here[0] != 0)
    def _():
        out[:, :width] = other
        out[:, width:] = mine


def total(here, keep, pair, core, both):
    return pl.pallas_call(
        total_body,
        out_shape=jax.ShapeDtypeStruct((keep.shape[0], 2 * keep.shape[1]), BF16),
        in_specs=[SMEM] + [VMEM] * 4,
        out_specs=VMEM,
        compiler_params=PARAMS,
        cost_estimate=COST,
        name="total",
    )(here, keep, pair, core, both)


def on_device(
    video_q,
    video_k,
    video_v,
    audio_k,
    audio_v,
    text_k,
    text_v,
    block_start,
    block_len,
    prompt_len,
    w_out,
):
    seq = lax.axis_index("seq")
    aud = lax.axis_index("aud")
    here = jnp.stack([seq % 2, (seq // 2) % 4, seq // 8, aud // 4, aud % 4]).astype(jnp.int32)

    own = stage(here, video_k, video_v, text_k, text_v)
    own_c = send(own, CORE)
    kv1 = send(own, X_A)
    kv2 = send(own, X_B)
    asked = send(video_q, Y_LO)
    lent = send(lend(here, audio_k, audio_v), Y_NEAR)
    came = send(w_out, Z_A)
    (near_mine,) = flash("near_mine", [own, own_c], [video_q])
    (near_other,) = flash("near_other", [own, own_c], [asked])
    kv1, kv2, near_mine, near_other, lent = lax.optimization_barrier(
        (kv1, kv2, near_mine, near_other, lent)
    )
    dealt = deal(here, audio_k, audio_v, lent)
    audios = [dealt[0], send(dealt[1], Z_A), send(dealt[2], Z_B), send(dealt[3], Z_2)]
    kv3 = send(kv1, X_A)
    kv1_c = send(kv1, CORE)
    kv2_c = send(kv2, CORE)
    mid_mine, mid_other = flash("mid", [kv1, kv2, kv1_c, kv2_c], [after(video_q, came), asked])
    w0, w1, w2 = split(here, w_out, after(came, *mid_mine))
    kv3, mid_mine, mid_other, w0, *audios = lax.optimization_barrier(
        (kv3, mid_mine, mid_other, w0, *audios)
    )
    w3 = send(w1, Z_A)
    w2 = send(w2, CORE)
    audios += [send(audio, CORE) for audio in audios]
    kv3_c = send(kv3, CORE)
    text = prompt(own, kv1, kv2, kv3)
    text_y = send(text, Y_LO)
    (packed,) = flash(
        "far_other", [kv3, kv3_c], [after(asked, *audios)], [[near_other, mid_other]], packed=True
    )
    got = send(packed, Y_LO)
    text_y = after(text_y, packed)
    text_yc = send(text_y, CORE)
    (far_mine,) = flash("far_mine", [kv3, kv3_c], [after(video_q, packed)], [[near_mine, mid_mine]])
    side_part = side(
        here,
        block_start,
        block_len,
        prompt_len,
        after(video_q, packed),
        audios,
        [own, kv1, kv2, kv3, own_c, kv1_c, kv2_c, kv3_c],
        [text_y, text_yc],
    )

    parts = join(here, far_mine, got, side_part)
    mine = [parts[0], send(parts[1], Z_A), send(parts[2], Z_B), send(parts[3], Z_2)]
    theirs = [send(part, CORE) for part in mine]
    keep, pair, cross, both = project(mine, theirs, [w0, w1, w2, w3])
    pair = send(pair, Y_HI)
    both = send(both, Y_HI_CORE)
    cross = send(cross, CORE)
    return total(here, keep, pair, cross, both)


def solution(mesh):
    placed = (
        P("seq", "aud"),
        P("seq", "aud"),
        P("seq", "aud"),
        P("aud", None),
        P("aud", None),
        P("seq", "aud"),
        P("seq", "aud"),
        P("seq"),
        P("seq"),
        P(),
        P("aud", None),
    )
    return jax.shard_map(
        on_device, mesh=mesh, in_specs=placed, out_specs=P(("seq", "aud"), None), check_vma=False
    )
```
